768 devices in a mesh: grp: 8 (over y), dev: 96 (over x, z, core).
Axes of the slice: x: 4, y: 8, z: 12, core: 2. Of those that a mesh axis runs over, the one named last changes fastest.
Arguments:
- sensitivity: float32 [768, 16, 128, 128], P(('grp', 'dev')), may hold values from -0.2 to 0.2
- tile_rows: int32 [768, 16], P(('grp', 'dev')), may hold values from 0 to 15
- tile_cols: int32 [768, 16], P(('grp', 'dev')), may hold values from 0 to 1535, as said below
- tile_count: int32 [768], P(('grp', 'dev')), may hold values from 1 to 16, as said below
- travel_times: float32 [12288, 128], P(('grp', 'dev')), may hold values from -6 to 6
Outputs:
- model_update: float32 [1536, 128], P(('grp', 'dev'))
- residual_ratio: float32 [1], replicated
The draws below stay inside these ranges and needn't reach their ends.
Inputs may be any that keep to these rules, and one draw needn't show every extreme that they name: `tile_cols`: A tile stored on a device of region g (its grp index) names a column block of the slabs of regions g - 1, g or g + 1, the slab of region h being blocks h * 192 to (h + 1) * 192 - 1. `tile_count`: some device has all 16 slots live.
All inputs are finite; a program needn't handle non-finite values.
Results may differ from the reference program's by a relative error of at most 0.0035.
Values sent between devices are 32-bit elements; how exact they have to be, the bound alone decides.
No kernel may reach another device: no remote copies, remote signals or barrier semaphores. Data moves between devices by JAX's collectives and lax.ppermute only.
A program may use at most 32 MiB of HBM per device.

```python
import jax
import jax.numpy as jnp
from jax import lax

TILE = 128
RB_DEV = 16
CB_DEV = 2
TS = 16
ITERS = 2
ROWBLOCKS = 12288
CELLBLOCKS = 1536
SLAB = 192
GROUPS = 8
DEVICES = 768


def draw_tile_count(key, part):
    key = jax.random.fold_in(key, 11)
    first_key, second_key = jax.random.split(key)
    levels = jax.random.randint(first_key, (DEVICES,), 0, TS + 1)
    counts = jnp.maximum(1, levels * levels // TS)
    chosen = jax.random.randint(second_key, (), 0, DEVICES)
    return jnp.where(jnp.arange(DEVICES) == chosen, TS, counts).astype(jnp.int32)


def draw_tile_cols(key, part):
    key = jax.random.fold_in(key, 12)
    first_key, second_key = jax.random.split(key)
    member_group = (jnp.arange(DEVICES) // (SLAB // CB_DEV))[:, None]
    offset = jax.random.randint(first_key, (DEVICES, TS), -1, 2)
    target = jnp.clip(member_group + offset, 0, GROUPS - 1)
    within = jax.random.randint(second_key, (DEVICES, TS), 0, SLAB)
    columns = target * SLAB + within
    columns = columns.at[DEVICES - 1, TS - 1].set(CELLBLOCKS - 1)
    return columns.astype(jnp.int32)


def with_ends(array, stream_key, smallest, top_value):
    extent = array.shape
    place = [jax.random.randint(jax.random.fold_in(stream_key, axis), (), 0, extent[axis]) for axis in range(len(extent))]
    array = array.at[tuple(place)].set(smallest)
    longest = extent.index(max(extent))
    place[longest] = (place[longest] + 1) % extent[longest]
    return array.at[tuple(place)].set(top_value)


def block_scale(key, extent, cuts, low, top_value):
    factor_of = 1.0
    for position, blocks in cuts:
        steps = jax.random.uniform(jax.random.fold_in(jax.random.fold_in(key, 6), position), (blocks,), jnp.float32, low / len(cuts), top_value / len(cuts))
        factor_of = factor_of * jnp.repeat(jnp.exp(steps), extent[position] // blocks).reshape((-1,) + (1,) * (len(extent) - 1 - position))
    return factor_of


def scatter_about(stream_key, extent, scale, limit, cuts=(), kind=jnp.bfloat16):
    level = block_scale(stream_key, extent, cuts, -0.22, 0.18) if cuts else 1.0
    array = jax.random.normal(stream_key, extent, jnp.float32) * scale * level
    return jnp.minimum(jnp.maximum(array, -limit), limit).astype(kind)


def setup_inputs(seed: int = 0) -> dict:
    key_of = jax.random.split(jax.random.key(seed), 6)
    return {
        "sensitivity": scatter_about(key_of[0], (DEVICES, TS, TILE, TILE), 0.03, 0.2, ((0, 768),), jnp.float32),
        "tile_rows": with_ends(jax.random.randint(key_of[1], (DEVICES, TS), 0, RB_DEV), jax.random.fold_in(key_of[1], 1), 0, RB_DEV - 1).astype(jnp.int32),
        "tile_cols": draw_tile_cols(jax.random.fold_in(key_of[5], 71), 0),
        "tile_count": draw_tile_count(jax.random.fold_in(key_of[5], 71), 0),
        "travel_times": scatter_about(key_of[4], (ROWBLOCKS, TILE), 1.0, 6.0, ((0, 768),), jnp.float32),
    }


def apply_forward(sensitivity, tile_rows, tile_cols, is_live, cell_vec):
    device_total = sensitivity.shape[0]
    picked = cell_vec[tile_cols]
    product = jnp.einsum('pkij,pkj->pki', sensitivity, picked, precision=lax.Precision.HIGHEST)
    product = jnp.where(is_live[:, :, None], product, jnp.float32(0.0))
    onehot = (tile_rows[:, None, :] == jnp.arange(RB_DEV, dtype=jnp.int32)[None, :, None]).astype(jnp.float32)
    row_sums = jnp.einsum('prk,pki->pri', onehot, product, precision=lax.Precision.HIGHEST)
    return row_sums.reshape(device_total * RB_DEV, TILE)

def apply_backward(sensitivity, tile_rows, tile_cols, is_live, ray_vec):
    device_total = sensitivity.shape[0]
    blocked = ray_vec.reshape(device_total, RB_DEV, TILE)
    picked = blocked[jnp.arange(device_total, dtype=jnp.int32)[:, None], tile_rows]
    product = jnp.einsum('pkij,pki->pkj', sensitivity, picked, precision=lax.Precision.HIGHEST)
    product = jnp.where(is_live[:, :, None], product, jnp.float32(0.0))
    return jax.ops.segment_sum(product.reshape(-1, TILE), tile_cols.reshape(-1), num_segments=CELLBLOCKS)

def reference(sensitivity, tile_rows, tile_cols, tile_count, travel_times):
    is_live = jnp.arange(TS, dtype=jnp.int32)[None, :] < tile_count[:, None]
    beta_first = jnp.sqrt(jnp.sum(travel_times * travel_times))
    ray_vec = travel_times / beta_first
    raw_cells = apply_backward(sensitivity, tile_rows, tile_cols, is_live, ray_vec)
    alpha_now = jnp.sqrt(jnp.sum(raw_cells * raw_cells))
    cell_vec = raw_cells / alpha_now
    direction = cell_vec
    solution = jnp.zeros_like(cell_vec)
    phi_bar = beta_first
    rho_bar = alpha_now
    for iteration in range(ITERS):
        residue = apply_forward(sensitivity, tile_rows, tile_cols, is_live, cell_vec) - alpha_now * ray_vec
        beta_now = jnp.sqrt(jnp.sum(residue * residue))
        ray_vec = residue / beta_now
        if iteration + 1 < ITERS:
            raw_cells = apply_backward(sensitivity, tile_rows, tile_cols, is_live, ray_vec) - beta_now * cell_vec
            alpha_next = jnp.sqrt(jnp.sum(raw_cells * raw_cells))
            cell_next = raw_cells / alpha_next
        rho_val = jnp.sqrt(rho_bar * rho_bar + beta_now * beta_now)
        cosine = rho_bar / rho_val
        sine_val = beta_now / rho_val
        phi_val = cosine * phi_bar
        phi_bar = sine_val * phi_bar
        solution = solution + phi_val / rho_val * direction
        if iteration + 1 < ITERS:
            rho_bar = -cosine * alpha_next
            direction = cell_next - sine_val * alpha_next / rho_val * direction
            cell_vec = cell_next
            alpha_now = alpha_next
    return (solution, (phi_bar / beta_first).reshape(1))
```

```python
import jax
import jax.numpy as jnp
from jax import lax
from jax.sharding import Mesh, PartitionSpec as P

NY, NX, NZ, NC = 8, 4, 12, 2
SLAB = 192
JB = SLAB // (NC * NZ)
SLOT = 3 * JB
LANES = 128
TABLE = NC * NZ * SLOT


def reduce_table(table, scalars, y):
    core = lax.axis_index("c")
    table = table.reshape(NC, NZ, SLOT, LANES)
    row = jnp.zeros((JB, LANES), jnp.float32)
    for i, value in enumerate(scalars):
        row = row.at[0, i].set(value)
    table = jnp.concatenate([table, jnp.broadcast_to(row, (NC, NZ, JB, LANES))], axis=2)
    pair = lax.all_gather(table, "c", axis=0, tiled=False)
    half = lax.dynamic_index_in_dim(pair, core, axis=1, keepdims=False).sum(0)
    part = lax.all_to_all(half, "z", 0, 0, tiled=True).sum(0)
    wide = lax.all_to_all(
        jnp.broadcast_to(part[None], (NY * NX, SLOT + JB, LANES)), ("y", "x"), 0, 0, tiled=True
    )
    wide = wide.reshape(NY, NX, 4, JB, LANES).sum(1)
    totals = wide[:, 3, 0].sum(0)
    near = lax.dynamic_slice_in_dim(
        jnp.pad(wide[:, :3], ((2, 2), (0, 0), (0, 0), (0, 0))), y, 5, axis=0
    )
    own = jnp.stack([near[d, 2] + near[d + 1, 1] + near[d + 2, 0] for d in range(3)]).reshape(SLOT, LANES)
    line = lax.all_to_all(jnp.broadcast_to(own[None], (NZ, SLOT, LANES)), "z", 0, 0, tiled=True)
    full = lax.all_gather(line, "c", axis=0, tiled=False)
    return full.reshape(TABLE, LANES), totals


def sum_all(scalars):
    row = jnp.zeros((1, LANES), jnp.float32)
    for i, value in enumerate(scalars):
        row = row.at[0, i].set(value)
    count = NY * NX * NC
    row = lax.all_to_all(jnp.broadcast_to(row[None], (count, 1, LANES)), ("y", "x", "c"), 0, 0, tiled=True).sum(0)
    row = lax.all_to_all(jnp.broadcast_to(row[None], (NZ, 1, LANES)), "z", 0, 0, tiled=True).sum(0)
    return row[0]


def local(sensitivity, tile_rows, tile_cols, tile_count, travel_times):
    tiles = sensitivity[0]
    row_ids = tile_rows[0]
    column_ids = tile_cols[0]
    live_count = tile_count[0]
    slots = tiles.shape[0]
    is_live = jnp.arange(slots, dtype=jnp.int32) < live_count
    row_onehot = (row_ids[None, :] == jnp.arange(travel_times.shape[0], dtype=jnp.int32)[:, None]).astype(jnp.float32)
    y = lax.axis_index("y")
    within = column_ids % SLAB
    position = (within // JB) * SLOT + (column_ids // SLAB - y + 1) * JB + within % JB
    mine = (lax.axis_index("x") * NZ + lax.axis_index("z")) * (2 * NC) + lax.axis_index("c") * 2
    mine = (mine // JB) * SLOT + JB + mine % JB

    def forward(cells):
        picked = jnp.take(cells, position, axis=0)
        product = jnp.einsum("kij,kj->ki", tiles, picked, precision=lax.Precision.HIGHEST)
        product = jnp.where(is_live[:, None], product, jnp.float32(0.0))
        return jnp.dot(row_onehot, product, precision=lax.Precision.HIGHEST)

    def backward(rays):
        picked = jnp.take(rays, row_ids, axis=0)
        product = jnp.einsum("kij,ki->kj", tiles, picked, precision=lax.Precision.HIGHEST)
        product = jnp.where(is_live[:, None], product, jnp.float32(0.0))
        return jax.ops.segment_sum(product, position, num_segments=TABLE)

    def own(cells):
        return lax.dynamic_slice_in_dim(cells, mine, 2, axis=0)

    cells_0, total = reduce_table(backward(travel_times), [jnp.sum(travel_times * travel_times)], y)
    beta_1 = jnp.sqrt(total[0])
    ray_1 = travel_times / beta_1
    raw_1 = cells_0 / beta_1
    image_1 = forward(raw_1)
    own_raw = own(raw_1)
    cells_1, total = reduce_table(
        backward(image_1),
        [jnp.sum(own_raw * own_raw), jnp.sum(image_1 * image_1), jnp.sum(image_1 * ray_1)],
        y,
    )
    alpha_1 = jnp.sqrt(total[0])
    beta_2 = jnp.sqrt(total[1] / total[0] - 2.0 * total[2] + total[0])
    ray_2 = (image_1 / alpha_1 - alpha_1 * ray_1) / beta_2
    raw_2 = (cells_1 / alpha_1 - alpha_1 * raw_1) / beta_2 - (beta_2 / alpha_1) * raw_1
    image_2 = forward(raw_2)
    own_raw_2 = own(raw_2)
    total = sum_all(
        [jnp.sum(own_raw_2 * own_raw_2), jnp.sum(image_2 * image_2), jnp.sum(image_2 * ray_2)]
    )
    alpha_2 = jnp.sqrt(total[0])
    beta_3 = jnp.sqrt(total[1] / total[0] - 2.0 * total[2] + total[0])
    direction = own_raw / alpha_1
    rho_1 = jnp.sqrt(alpha_1 * alpha_1 + beta_2 * beta_2)
    cosine, sine = alpha_1 / rho_1, beta_2 / rho_1
    update = (cosine * beta_1 / rho_1) * direction
    phi_bar = sine * beta_1
    rho_bar = -cosine * alpha_2
    direction = own_raw_2 / alpha_2 - (sine * alpha_2 / rho_1) * direction
    rho_2 = jnp.sqrt(rho_bar * rho_bar + beta_3 * beta_3)
    cosine, sine = rho_bar / rho_2, beta_3 / rho_2
    update = update + (cosine * phi_bar / rho_2) * direction
    phi_bar = sine * phi_bar
    return update, (phi_bar / beta_1).reshape(1)


def solution(mesh):
    split = Mesh(mesh.devices.reshape(NY, NX, NZ, NC), ("y", "x", "z", "c"))
    every = P(("y", "x", "z", "c"))
    return jax.shard_map(
        local, mesh=split, in_specs=(every,) * 5, out_specs=(every, P()), check_vma=False
    )
```

```python
import jax
import jax.numpy as jnp
from jax import lax
from jax.experimental import pallas as pl
from jax.experimental.pallas import tpu as pltpu
from jax.sharding import Mesh, PartitionSpec as P

NY, NX, NZ, NC = 8, 4, 12, 2
SLAB = 192
JB = SLAB // (NC * NZ)
SLOT = 3 * JB
WIDE = SLOT + JB
LANES = 128
TABLE = NC * NZ * SLOT
TS = 16
RB = 16
VM = pl.BlockSpec(memory_space=pltpu.VMEM)
SM = pl.BlockSpec(memory_space=pltpu.SMEM)


def shape(*dims):
    return jax.ShapeDtypeStruct(dims, jnp.float32)


def call(kernel, outs, ins, args, scratch=()):
    return pl.pallas_call(
        kernel,
        out_shape=outs,
        in_specs=ins,
        out_specs=jax.tree.map(lambda _: VM, outs),
        scratch_shapes=scratch,
        compiler_params=pltpu.CompilerParams(vmem_limit_bytes=32 * 1024 * 1024),
    )(*args)


def live(ids, k):
    return jnp.where(k < ids[3, 0], jnp.float32(1.0), jnp.float32(0.0))


def total(value):
    return jnp.sum(jnp.sum(value, axis=0, keepdims=True), axis=1, keepdims=True)


def packed(values):
    lane = lax.broadcasted_iota(jnp.int32, (1, LANES), 1)
    row = jnp.zeros((1, LANES), jnp.float32)
    for i, value in enumerate(values):
        row = jnp.where(lane == i, value, row)
    return row


def backward_terms(ids, tiles, columns, table, where):
    for k in range(TS):
        term = jnp.sum(tiles[k] * columns[ids[0, k]], axis=0, keepdims=True) * live(ids, k)
        at = pl.ds(ids[where, k], 1)
        table[at, :] = table[at, :] + term


def first_kernel(ids, tiles, times, table, times_t, columns):
    padded = jnp.concatenate([times[...], jnp.zeros((LANES - RB, LANES), jnp.float32)], axis=0)
    turned = padded.T
    times_t[...] = turned
    for r in range(RB):
        columns[r] = jnp.broadcast_to(turned[:, r : r + 1], (LANES, LANES))
    table[...] = jnp.zeros_like(table)
    backward_terms(ids, tiles, columns, table, 1)


def second_kernel(ids, tiles, cells, times_t, table, image_t, columns):
    columns[...] = jnp.zeros_like(columns)
    for k in range(TS):
        term = jnp.sum(tiles[k] * cells[pl.ds(ids[1, k], 1), :], axis=1, keepdims=True) * live(ids, k)
        r = ids[0, k]
        columns[r] = columns[r] + term
    lane = lax.broadcasted_iota(jnp.int32, (LANES, LANES), 1)
    image = jnp.zeros((LANES, LANES), jnp.float32)
    for r in range(RB):
        image = jnp.where(lane == r, columns[r], image)
    image_t[...] = image
    table[...] = jnp.zeros_like(table)
    backward_terms(ids, tiles, columns, table, 2)
    times = times_t[...]
    own = cells[pl.ds(ids[3, 1], 2), :]
    row = packed([total(times * times), total(own * own), total(image * image), total(image * times)])
    for s in range(NC * NZ):
        table[s * WIDE + SLOT : s * WIDE + SLOT + 1, :] = row


def norms(sums):
    times_2, cells_2, image_2, cross = (sums[:, i : i + 1] for i in range(4))
    beta_1 = jnp.sqrt(times_2)
    square = cells_2 / times_2
    alpha_1 = jnp.sqrt(square)
    beta_2 = jnp.sqrt(image_2 / cells_2 - 2.0 * (cross / times_2) + square)
    return beta_1, alpha_1, beta_2


def third_kernel(ids, tiles, cells, cells_2, times_t, image_t, sums, rows, own_raw):
    beta_1, alpha_1, beta_2 = norms(sums[...])
    scale = 1.0 / (beta_1 * alpha_1 * beta_2)
    shift = (alpha_1 / beta_2 + beta_2 / alpha_1) / beta_1
    lane = lax.broadcasted_iota(jnp.int32, (LANES, LANES), 1)
    image = jnp.zeros((LANES, LANES), jnp.float32)
    for k in range(TS):
        at = pl.ds(ids[1, k], 1)
        raw = scale * cells_2[at, :] - shift * cells[at, :]
        term = jnp.sum(tiles[k] * raw, axis=1, keepdims=True) * live(ids, k)
        image = image + jnp.where(lane == ids[0, k], term, 0.0)
    ray = (image_t[...] / (alpha_1 * beta_1) - (alpha_1 / beta_1) * times_t[...]) / beta_2
    at = pl.ds(ids[3, 1], 2)
    own_1 = cells[at, :]
    own_2 = scale * cells_2[at, :] - shift * own_1
    own_raw[0] = own_1 / beta_1
    own_raw[1] = own_2
    row = packed([total(own_2 * own_2), total(image * image), total(image * ray)])
    rows[...] = jnp.broadcast_to(row[None], rows.shape)


def last_kernel(rows, sums, own_raw, update, ratio):
    beta_1, alpha_1, beta_2 = norms(sums[...])
    row = jnp.sum(rows[...], axis=0)
    cells_2, image_2, cross = (row[:, i : i + 1] for i in range(3))
    alpha_2 = jnp.sqrt(cells_2)
    beta_3 = jnp.sqrt(image_2 / cells_2 - 2.0 * cross + cells_2)
    direction = own_raw[0] / alpha_1
    rho_1 = jnp.sqrt(alpha_1 * alpha_1 + beta_2 * beta_2)
    cosine, sine = alpha_1 / rho_1, beta_2 / rho_1
    found = (cosine * beta_1 / rho_1) * direction
    phi_bar = sine * beta_1
    rho_bar = -cosine * alpha_2
    direction = own_raw[1] / alpha_2 - (sine * alpha_2 / rho_1) * direction
    rho_2 = jnp.sqrt(rho_bar * rho_bar + beta_3 * beta_3)
    cosine, sine = rho_bar / rho_2, beta_3 / rho_2
    update[...] = found + (cosine * phi_bar / rho_2) * direction
    ratio[...] = sine * phi_bar / beta_1


def line_kernel(parts, copies):
    total_part = parts[0]
    for z in range(1, NZ):
        total_part = total_part + parts[z]
    for s in range(NY * NX):
        copies[s] = total_part


def plane_kernel(ids, parts, copies, *sums):
    y = ids[3, 2]
    for d in range(3):
        acc = jnp.zeros((JB, LANES), jnp.float32)
        for e in range(3):
            other = y + (d - 1) + (e - 1)
            inside = jnp.logical_and(other >= 0, other < NY)
            base = jnp.clip(other, 0, NY - 1) * NX
            rel = 2 - e
            term = parts[base, rel * JB : (rel + 1) * JB, :]
            for x in range(1, NX):
                term = term + parts[base + x, rel * JB : (rel + 1) * JB, :]
            acc = acc + jnp.where(inside, term, 0.0)
        for z in range(NZ):
            copies[z, d * JB : (d + 1) * JB, :] = acc
    if sums:
        row = parts[0, SLOT : SLOT + 1, :]
        for s in range(1, NY * NX):
            row = row + parts[s, SLOT : SLOT + 1, :]
        sums[0][...] = row


def exchange(table, ids, depth):
    core = lax.axis_index("c")
    pair = lax.all_gather(table.reshape(NC, NZ, depth, LANES), "c", axis=0, tiled=False)
    half = lax.dynamic_index_in_dim(pair, core, axis=1, keepdims=False).sum(0)
    parts = lax.all_to_all(half, "z", 0, 0, tiled=True)
    copies = call(line_kernel, shape(NY * NX, depth, LANES), [VM], (parts,))
    parts = lax.all_to_all(copies, ("y", "x"), 0, 0, tiled=True)
    outs = [shape(NZ, SLOT, LANES)] + ([shape(1, LANES)] if depth > SLOT else [])
    copies, *sums = call(plane_kernel, outs, [SM, VM], (ids, parts))
    line = lax.all_to_all(copies, "z", 0, 0, tiled=True)
    full = lax.all_gather(line, "c", axis=0, tiled=False)
    return full.reshape(TABLE, LANES), *sums


def local(sensitivity, tile_rows, tile_cols, tile_count, travel_times):
    tiles = sensitivity[0]
    columns = tile_cols[0]
    y = lax.axis_index("y")
    within = columns % SLAB
    slot = within // JB
    offset = jnp.clip(columns // SLAB - y + 1, 0, 2) * JB + within % JB
    mine = (lax.axis_index("x") * NZ + lax.axis_index("z")) * (2 * NC) + lax.axis_index("c") * 2
    mine = (mine // JB) * SLOT + JB + mine % JB
    place = jnp.arange(TS, dtype=jnp.int32)
    facts = jnp.where(place == 0, tile_count[0], jnp.where(place == 1, mine, y))
    ids = jnp.stack([jnp.clip(tile_rows[0], 0, RB - 1), slot * SLOT + offset, slot * WIDE + offset, facts])
    square = shape(LANES, LANES)
    scratch = [pltpu.VMEM((RB, LANES, LANES), jnp.float32)]

    table, times_t = call(
        first_kernel, [shape(TABLE, LANES), square], [SM, VM, VM], (ids, tiles, travel_times), scratch
    )
    (cells,) = exchange(table, ids, SLOT)
    table, image_t = call(
        second_kernel,
        [shape(NC * NZ * WIDE, LANES), square],
        [SM, VM, VM, VM],
        (ids, tiles, cells, times_t),
        scratch,
    )
    cells_2, sums = exchange(table, ids, WIDE)
    count = NY * NX * NC
    rows, own_raw = call(
        third_kernel,
        [shape(count, 1, LANES), shape(2, 2, LANES)],
        [SM] + [VM] * 6,
        (ids, tiles, cells, cells_2, times_t, image_t, sums),
    )
    rows = lax.all_to_all(rows, ("y", "x", "c"), 0, 0, tiled=True)
    rows = jnp.broadcast_to(rows.sum(0)[None], (NZ, 1, LANES))
    rows = lax.all_to_all(rows, "z", 0, 0, tiled=True)
    update, ratio = call(last_kernel, [shape(2, LANES), shape(1, 1)], [VM] * 3, (rows, sums, own_raw))
    return update, ratio.reshape(1)


def solution(mesh):
    split = Mesh(mesh.devices.reshape(NY, NX, NZ, NC), ("y", "x", "z", "c"))
    every = P(("y", "x", "z", "c"))
    return jax.shard_map(
        local, mesh=split, in_specs=(every,) * 5, out_specs=(every, P()), check_vma=False
    )
```

```python
import jax
import jax.numpy as jnp
from jax import lax
from jax.experimental import pallas as pl
from jax.experimental.pallas import tpu as pltpu
from jax.sharding import Mesh, PartitionSpec as P

NY, NX, NZ, NC = 8, 4, 12, 2
NH = 2
SLAB = 192
SLOTS = NH * NZ
JB = SLAB // (NC * SLOTS)
SLOT = 3 * JB
DEPTH = 4 * JB
LANES = 128
TABLE = NC * SLOTS * DEPTH
TS = 16
RB = 16
VM = pl.BlockSpec(memory_space=pltpu.VMEM)
SM = pl.BlockSpec(memory_space=pltpu.SMEM)


def shape(*dims):
    return jax.ShapeDtypeStruct(dims, jnp.float32)


def call(kernel, outs, ins, args, scratch=()):
    return pl.pallas_call(
        kernel,
        out_shape=outs,
        in_specs=ins,
        out_specs=jax.tree.map(lambda _: VM, outs),
        scratch_shapes=scratch,
        compiler_params=pltpu.CompilerParams(vmem_limit_bytes=32 * 1024 * 1024),
    )(*args)


def coordinates():
    me = lax.axis_index("all")
    y = me // (NX * NZ * NC)
    rest = me - y * (NX * NZ * NC)
    return y, rest // NC, rest % NC


def device(y, x, z, c):
    return ((y * NX + x) * NZ + z) * NC + c


PAIRS = [[device(y, x, z, 0), device(y, x, z, 1)] for y in range(NY) for x in range(NX) for z in range(NZ)]
LINES = [
    [device(y, x, z, c) for x in pair for z in range(NZ)]
    for y in range(NY)
    for pair in ((0, 1), (3, 2))
    for c in range(NC)
]
PLANES = [
    [device(y, x, z, c) for x in pair for y in range(NY)]
    for z in range(NZ)
    for pair in ((0, 3), (1, 2))
    for c in range(NC)
]
CHIPS_Z = [
    [device(y, x, z, c) for z in range(NZ) for c in range(NC)] for y in range(NY) for x in range(NX)
]
ALL_YX = [
    [device(y, x, z, c) for y in range(NY) for x in range(NX)] for z in range(NZ) for c in range(NC)
]


def swap(array, groups):
    return lax.all_to_all(array, "all", 0, 0, tiled=True, axis_index_groups=groups)


def placed(k, rows, cols, count):
    y, _, _ = coordinates()
    column = cols[0, k]
    region = column // SLAB
    within = column - region * SLAB
    slot = within // JB
    band = jnp.clip(region - y + 1, 0, 2)
    at = jnp.clip(slot * DEPTH + band * JB + (within - slot * JB), 0, TABLE - 1)
    return jnp.clip(rows[0, k], 0, RB - 1), at, jnp.where(k < count[0], jnp.float32(1.0), jnp.float32(0.0))


def own_rows(cells):
    _, slot, core = coordinates()
    return cells[pl.ds(slot * DEPTH + JB + core * 2, 2), :]


def total(value):
    return jnp.sum(jnp.sum(value, axis=0, keepdims=True), axis=1, keepdims=True)


def packed(values):
    lane = lax.broadcasted_iota(jnp.int32, (1, LANES), 1)
    row = jnp.zeros((1, LANES), jnp.float32)
    for i, value in enumerate(values):
        row = jnp.where(lane == i, value, row)
    return row


def backward_terms(places, tiles, columns, table, row):
    spare = jnp.broadcast_to(row, (JB, LANES))
    block = jnp.concatenate([jnp.zeros((SLOT, LANES), jnp.float32), spare], axis=0)
    for s in range(NC * SLOTS):
        table[s * DEPTH : (s + 1) * DEPTH, :] = block
    for k, (r, at, weight) in enumerate(places):
        term = jnp.sum(tiles[k] * columns[r], axis=0, keepdims=True) * weight
        table[pl.ds(at, 1), :] = table[pl.ds(at, 1), :] + term


def first_kernel(rows, cols, count, tiles_far, times, table, times_t, columns, tiles, sem):
    copy = pltpu.make_async_copy(tiles_far, tiles, sem)
    copy.start()
    padded = jnp.concatenate([times[...], jnp.zeros((LANES - RB, LANES), jnp.float32)], axis=0)
    turned = padded.T
    times_t[...] = turned
    for r in range(RB):
        columns[r] = jnp.broadcast_to(turned[:, r : r + 1], (LANES, LANES))
    places = [placed(k, rows, cols, count) for k in range(TS)]
    copy.wait()
    backward_terms(places, tiles, columns, table, packed([total(turned * turned)]))


def second_kernel(rows, cols, count, tiles, cells, times_t, sums, table, image_t, columns):
    inverse = 1.0 / jnp.sqrt(sums[:, 0:1])
    places = [placed(k, rows, cols, count) for k in range(TS)]
    columns[...] = jnp.zeros_like(columns)
    for k, (r, at, weight) in enumerate(places):
        raw = cells[pl.ds(at, 1), :] * inverse
        term = jnp.sum(tiles[k] * raw, axis=1, keepdims=True) * weight
        columns[r] = columns[r] + term
    lane = lax.broadcasted_iota(jnp.int32, (LANES, LANES), 1)
    image = jnp.zeros((LANES, LANES), jnp.float32)
    for r in range(RB):
        image = jnp.where(lane == r, columns[r], image)
    image_t[...] = image
    ray = times_t[...] * inverse
    own = own_rows(cells) * inverse
    row = packed([total(own * own), total(image * image), total(image * ray)])
    backward_terms(places, tiles, columns, table, row)


def norms(sums):
    square, image_2, cross = (sums[:, i : i + 1] for i in range(3))
    return jnp.sqrt(square), jnp.sqrt(image_2 / square - 2.0 * cross + square)


def third_kernel(rows, cols, count, tiles, cells, cells_2, times_t, image_t, sums, sums_2, copies, own_raw):
    inverse = 1.0 / jnp.sqrt(sums[:, 0:1])
    alpha_1, beta_2 = norms(sums_2)
    scale = 1.0 / (alpha_1 * beta_2)
    shift = (alpha_1 / beta_2 + beta_2 / alpha_1) * inverse
    lane = lax.broadcasted_iota(jnp.int32, (LANES, LANES), 1)
    image = jnp.zeros((LANES, LANES), jnp.float32)
    for k in range(TS):
        r, at, weight = placed(k, rows, cols, count)
        raw = scale * cells_2[pl.ds(at, 1), :] - shift * cells[pl.ds(at, 1), :]
        term = jnp.sum(tiles[k] * raw, axis=1, keepdims=True) * weight
        image = image + jnp.where(lane == r, term, 0.0)
    ray = (image_t[...] / alpha_1 - (alpha_1 * inverse) * times_t[...]) / beta_2
    own_1 = own_rows(cells)
    own_2 = scale * own_rows(cells_2) - shift * own_1
    own_raw[0] = own_1 * inverse
    own_raw[1] = own_2
    row = packed([total(own_2 * own_2), total(image * image), total(image * ray)])
    copies[...] = jnp.broadcast_to(row[None], copies.shape)


def last_kernel(rows, sums, sums_2, own_raw, update, ratio):
    beta_1 = jnp.sqrt(sums[:, 0:1])
    alpha_1, beta_2 = norms(sums_2)
    row = jnp.sum(rows[...], axis=0)
    alpha_2, beta_3 = norms(row)
    direction = own_raw[0] / alpha_1
    rho_1 = jnp.sqrt(alpha_1 * alpha_1 + beta_2 * beta_2)
    cosine, sine = alpha_1 / rho_1, beta_2 / rho_1
    found = (cosine * beta_1 / rho_1) * direction
    phi_bar = sine * beta_1
    rho_bar = -cosine * alpha_2
    direction = own_raw[1] / alpha_2 - (sine * alpha_2 / rho_1) * direction
    rho_2 = jnp.sqrt(rho_bar * rho_bar + beta_3 * beta_3)
    cosine, sine = rho_bar / rho_2, beta_3 / rho_2
    update[...] = found + (cosine * phi_bar / rho_2) * direction
    ratio[...] = sine * phi_bar / beta_1


def line_kernel(parts, copies):
    part = parts[0]
    for s in range(1, SLOTS):
        part = part + parts[s]
    for s in range(NY * NH):
        copies[s] = part


def plane_kernel(parts, copies, sums):
    y, _, _ = coordinates()
    bands = []
    for d in range(3):
        acc = jnp.zeros((JB, LANES), jnp.float32)
        for e in range(3):
            other = y + (d + e - 2)
            inside = jnp.logical_and(other >= 0, other < NY)
            other = jnp.clip(other, 0, NY - 1)
            rel = (2 - e) * JB
            term = parts[other, rel : rel + JB, :] + parts[other + NY, rel : rel + JB, :]
            acc = acc + jnp.where(inside, term, 0.0)
        bands.append(acc)
    row = parts[0, SLOT : SLOT + 1, :]
    for s in range(1, NY * NH):
        row = row + parts[s, SLOT : SLOT + 1, :]
    sums[...] = row
    block = jnp.concatenate(bands + [jnp.zeros((DEPTH - SLOT, LANES), jnp.float32)], axis=0)
    for s in range(SLOTS):
        copies[s] = block


def exchange(table):
    _, _, core = coordinates()
    pair = lax.all_gather(table.reshape(NC, SLOTS, DEPTH, LANES), "all", axis=0, axis_index_groups=PAIRS)
    half = lax.dynamic_index_in_dim(pair, core, axis=1, keepdims=False).sum(0)
    copies = call(line_kernel, shape(NY * NH, DEPTH, LANES), [VM], (swap(half, LINES),))
    copies, sums = call(
        plane_kernel, [shape(SLOTS, DEPTH, LANES), shape(1, LANES)], [VM], (swap(copies, PLANES),)
    )
    full = lax.all_gather(swap(copies, LINES), "all", axis=0, axis_index_groups=PAIRS)
    return full.reshape(TABLE, LANES), sums


def local(sensitivity, tile_rows, tile_cols, tile_count, travel_times):
    tiles = sensitivity[0]
    lists = (tile_rows, tile_cols, tile_count)
    square = shape(LANES, LANES)
    columns = pltpu.VMEM((RB, LANES, LANES), jnp.float32)
    far = pl.BlockSpec(memory_space=pl.ANY)

    table, times_t = call(
        first_kernel,
        [shape(TABLE, LANES), square],
        [SM] * 3 + [far, VM],
        (*lists, tiles, travel_times),
        [columns, columns, pltpu.SemaphoreType.DMA],
    )
    cells, sums = exchange(table)
    table, image_t = call(
        second_kernel,
        [shape(TABLE, LANES), square],
        [SM] * 3 + [VM] * 4,
        (*lists, tiles, cells, times_t, sums),
        [columns],
    )
    cells_2, sums_2 = exchange(table)
    copies, own_raw = call(
        third_kernel,
        [shape(NZ * NC, 1, LANES), shape(2, 2, LANES)],
        [SM] * 3 + [VM] * 7,
        (*lists, tiles, cells, cells_2, times_t, image_t, sums, sums_2),
    )
    rows = swap(copies, CHIPS_Z).sum(0)
    rows = swap(jnp.broadcast_to(rows[None], (NY * NX, 1, LANES)), ALL_YX)
    update, ratio = call(last_kernel, [shape(2, LANES), shape(1, 1)], [VM] * 4, (rows, sums, sums_2, own_raw))
    return update, ratio.reshape(1)


def solution(mesh):
    flat = Mesh(mesh.devices.reshape(-1), ("all",))
    every = P("all")
    return jax.shard_map(
        local, mesh=flat, in_specs=(every,) * 5, out_specs=(every, P()), check_vma=False
    )
```

```python
import jax
import jax.numpy as jnp
from jax import lax
from jax.experimental import pallas as pl
from jax.experimental.pallas import tpu as pltpu
from jax.sharding import Mesh, PartitionSpec as P

NY, NX, NZ, NC = 8, 4, 12, 2
NH = 2
SLAB = 192
SLOTS = NH * NZ
JB = SLAB // (NC * SLOTS)
SLOT = 3 * JB
NARROW = (3, JB)
PAIRED = (SLOT // 2 + 1, 2)
LANES = 128
TABLE = NC * SLOTS
TS = 16
RB = 16
VM = pl.BlockSpec(memory_space=pltpu.VMEM)
SM = pl.BlockSpec(memory_space=pltpu.SMEM)


def shape(*dims):
    return jax.ShapeDtypeStruct(dims, jnp.float32)


def call(kernel, outs, ins, args, scratch=()):
    return pl.pallas_call(
        kernel,
        out_shape=outs,
        in_specs=ins,
        out_specs=jax.tree.map(lambda _: VM, outs),
        scratch_shapes=scratch,
        compiler_params=pltpu.CompilerParams(vmem_limit_bytes=32 * 1024 * 1024),
    )(*args)


def over_slab(value):
    return (value * 43691) >> 23


def coordinates():
    me = lax.axis_index("all")
    y = over_slab(2 * me)
    rest = me - y * (NX * NZ * NC)
    return y, rest >> 1, rest & 1


def device(y, x, z, c):
    return ((y * NX + x) * NZ + z) * NC + c


PAIRS = [[device(y, x, z, 0), device(y, x, z, 1)] for y in range(NY) for x in range(NX) for z in range(NZ)]
LINES = [
    [device(y, x, z, c) for x in pair for z in range(NZ)]
    for y in range(NY)
    for pair in ((0, 1), (3, 2))
    for c in range(NC)
]
PLANES = [
    [device(y, x, z, c) for x in pair for y in range(NY)]
    for z in range(NZ)
    for pair in ((0, 3), (1, 2))
    for c in range(NC)
]
CHIPS_Z = [
    [device(y, x, z, c) for z in range(NZ) for c in range(NC)] for y in range(NY) for x in range(NX)
]
ALL_YX = [
    [device(y, x, z, c) for y in range(NY) for x in range(NX)] for z in range(NZ) for c in range(NC)
]


def swap(array, groups):
    return lax.all_to_all(array, "all", 0, 0, tiled=True, axis_index_groups=groups)


def placed(lists):
    rows, cols, count = lists
    y, _, _ = coordinates()
    places = []
    for k in range(TS):
        column = cols[0, k]
        region = over_slab(column)
        within = column - region * SLAB
        slot = jnp.clip(within >> 2, 0, TABLE - 1)
        at = jnp.clip(region - y + 1, 0, 2) * JB + (within & 3)
        weight = jnp.where(k < count[0, 0], jnp.float32(1.0), jnp.float32(0.0))
        places.append((jnp.clip(rows[0, k], 0, RB - 1), slot, at, weight))
    return places


def picked(cells, slot, at):
    return cells[slot, at >> 2, pl.ds(at & 3, 1), :]


def own_rows(cells):
    _, slot, core = coordinates()
    return cells[slot, 1, pl.ds(core * 2, 2), :]


def total(value):
    return jnp.sum(jnp.sum(value, axis=0, keepdims=True), axis=1, keepdims=True)


def packed(values):
    lane = lax.broadcasted_iota(jnp.int32, (1, LANES), 1)
    row = jnp.zeros((1, LANES), jnp.float32)
    for i, value in enumerate(values):
        row = jnp.where(lane == i, value, row)
    return row


def backward_terms(places, tiles, columns, table):
    shift = 2 if table.shape[2] == JB else 1
    for k, (r, slot, at, weight) in enumerate(places):
        term = jnp.sum(tiles[k] * columns[r], axis=0, keepdims=True) * weight
        row = pl.ds(at & (table.shape[2] - 1), 1)
        table[slot, at >> shift, row, :] = table[slot, at >> shift, row, :] + term


def first_kernel(rows, cols, count, tiles, times, table, times_t, columns):
    padded = jnp.concatenate([times[...], jnp.zeros((LANES - RB, LANES), jnp.float32)], axis=0)
    turned = padded.T
    times_t[...] = turned
    for r in range(RB):
        columns[r] = jnp.broadcast_to(turned[:, r : r + 1], (LANES, LANES))
    table[...] = jnp.zeros_like(table)
    backward_terms(placed((rows, cols, count)), tiles, columns, table)


def second_kernel(rows, cols, count, tiles, cells, times_t, table, image_t, columns):
    places = placed((rows, cols, count))
    columns[...] = jnp.zeros_like(columns)
    table[...] = jnp.zeros_like(table)
    for k, (r, slot, at, weight) in enumerate(places):
        term = jnp.sum(tiles[k] * picked(cells, slot, at), axis=1, keepdims=True) * weight
        columns[r] = columns[r] + term
    lane = lax.broadcasted_iota(jnp.int32, (LANES, LANES), 1)
    image = jnp.zeros((LANES, LANES), jnp.float32)
    for r in range(RB):
        image = jnp.where(lane == r, columns[r], image)
    image_t[...] = image
    times = times_t[...]
    own = own_rows(cells)
    row = packed([total(times * times), total(own * own), total(image * image), total(image * times)])
    row = jnp.broadcast_to(row, (2, LANES))
    for s in range(TABLE):
        table[s, SLOT // 2] = row
    backward_terms(places, tiles, columns, table)


def third_kernel(rows, cols, count, tiles, cells, cells_2, times_t, image_t, sums, copies, held):
    times_sum, cells_sum, image_sum, cross = (sums[:, i : i + 1] for i in range(4))
    beta_1 = jnp.sqrt(times_sum)
    square = cells_sum / times_sum
    alpha_1 = jnp.sqrt(square)
    beta_2 = jnp.sqrt(image_sum / cells_sum - 2.0 * (cross / times_sum) + square)
    scale = 1.0 / (beta_1 * alpha_1 * beta_2)
    shift = (alpha_1 / beta_2 + beta_2 / alpha_1) / beta_1
    lane = lax.broadcasted_iota(jnp.int32, (LANES, LANES), 1)
    image = jnp.zeros((LANES, LANES), jnp.float32)
    for k, (r, slot, at, weight) in enumerate(placed((rows, cols, count))):
        raw = scale * picked(cells_2, slot, at) - shift * picked(cells, slot, at)
        term = jnp.sum(tiles[k] * raw, axis=1, keepdims=True) * weight
        image = image + jnp.where(lane == r, term, 0.0)
    ray = (image_t[...] / (alpha_1 * beta_1) - (alpha_1 / beta_1) * times_t[...]) / beta_2
    own_1 = own_rows(cells)
    own_2 = scale * own_rows(cells_2) - shift * own_1
    row = packed([total(own_2 * own_2), total(image * image), total(image * ray)])
    copies[...] = jnp.broadcast_to(row[None], copies.shape)
    rho_1 = jnp.sqrt(alpha_1 * alpha_1 + beta_2 * beta_2)
    cosine, sine = alpha_1 / rho_1, beta_2 / rho_1
    direction = own_1 / (beta_1 * alpha_1)
    held[0] = own_2
    held[1] = (cosine * beta_1 / rho_1) * direction
    held[2] = (sine / rho_1) * direction
    for i, value in enumerate([cosine, sine, sine * beta_1]):
        held[3 + i] = jnp.broadcast_to(value, (2, LANES))


def last_kernel(rows, held, update, ratio):
    cells_sum, image_sum, cross = (jnp.sum(rows[:, :, i : i + 1], axis=0) for i in range(3))
    alpha_2 = jnp.sqrt(cells_sum)
    beta_3 = jnp.sqrt(image_sum / cells_sum - 2.0 * cross + cells_sum)
    direction = held[0] / alpha_2 - alpha_2 * held[2]
    rho_bar = -held[3] * alpha_2
    rho_2 = jnp.sqrt(rho_bar * rho_bar + beta_3 * beta_3)
    update[...] = held[1] + (rho_bar / rho_2 * held[5] / rho_2) * direction
    ratio[...] = (beta_3 / rho_2[0:1, 0:1]) * held[4][0:1, 0:1]


def line_kernel(parts, copies):
    part = parts[0]
    for s in range(1, SLOTS):
        part = part + parts[s]
    for s in range(NY * NH):
        copies[s] = part


def plane_kernel(parts, copies, *sums):
    y, _, _ = coordinates()
    width = parts.shape[2]
    for d in range(3):
        for i in range(JB // width):
            acc = jnp.zeros((width, LANES), jnp.float32)
            for e in range(3):
                other = y + (d + e - 2)
                inside = jnp.logical_and(other >= 0, other < NY)
                other = jnp.clip(other, 0, NY - 1)
                at = (2 - e) * (JB // width) + i
                acc = acc + jnp.where(inside, parts[other, at] + parts[other + NY, at], 0.0)
            for s in range(SLOTS):
                copies[s, d, i * width : (i + 1) * width, :] = acc
    if sums:
        row = parts[0, SLOT // 2]
        for s in range(1, NY * NH):
            row = row + parts[s, SLOT // 2]
        sums[0][...] = row[0:1, :]


def exchange(table):
    _, _, core = coordinates()
    slot = table.shape[1:]
    pair = lax.all_gather(table.reshape((NC, SLOTS) + slot), "all", axis=0, axis_index_groups=PAIRS)
    half = lax.dynamic_index_in_dim(pair, core, axis=1, keepdims=False).sum(0)
    copies = call(line_kernel, shape(NY * NH, *slot), [VM], (swap(half, LINES),))
    outs = [shape(SLOTS, *NARROW, LANES)] + [shape(1, LANES)] * (slot[1] != JB)
    copies, *sums = call(plane_kernel, outs, [VM], (swap(copies, PLANES),))
    full = lax.all_gather(swap(copies, LINES), "all", axis=0, axis_index_groups=PAIRS)
    return full.reshape(TABLE, *NARROW, LANES), *sums


def local(sensitivity, tile_rows, tile_cols, tile_count, travel_times):
    tiles = sensitivity[0]
    lists = (tile_rows, tile_cols, tile_count.reshape(1, 1))
    square = shape(LANES, LANES)
    columns = pltpu.VMEM((RB, LANES, LANES), jnp.float32)

    table, times_t = call(
        first_kernel,
        [shape(TABLE, *NARROW, LANES), square],
        [SM] * 3 + [VM] * 2,
        (*lists, tiles, travel_times),
        [columns],
    )
    (cells,) = exchange(table)
    table, image_t = call(
        second_kernel,
        [shape(TABLE, *PAIRED, LANES), square],
        [SM] * 3 + [VM] * 3,
        (*lists, tiles, cells, times_t),
        [columns],
    )
    cells_2, sums = exchange(table)
    copies, held = call(
        third_kernel,
        [shape(NZ * NC, 1, LANES), shape(6, 2, LANES)],
        [SM] * 3 + [VM] * 6,
        (*lists, tiles, cells, cells_2, times_t, image_t, sums),
    )
    rows = swap(copies, CHIPS_Z).sum(0)
    rows = swap(jnp.broadcast_to(rows[None], (NY * NX, 1, LANES)), ALL_YX)
    update, ratio = call(last_kernel, [shape(2, LANES), shape(1, 1)], [VM] * 2, (rows, held))
    return update, ratio.reshape(1)


def solution(mesh):
    flat = Mesh(mesh.devices.reshape(-1), ("all",))
    every = P("all")
    return jax.shard_map(
        local, mesh=flat, in_specs=(every,) * 5, out_specs=(every, P()), check_vma=False
    )
```

```python
import jax
import jax.numpy as jnp
from jax import lax
from jax.experimental import pallas as pl
from jax.experimental.pallas import tpu as pltpu
from jax.sharding import Mesh, PartitionSpec as P

NY, NX, NZ, NC = 8, 4, 12, 2
NH = 2
SLAB = 192
SLOTS = NH * NZ
JB = SLAB // (NC * SLOTS)
SLOT = 3 * JB
NARROW = (3, JB)
PAIRED = (SLOT // 2 + 1, 2)
LANES = 128
TABLE = NC * SLOTS
TS = 16
RB = 16
VM = pl.BlockSpec(memory_space=pltpu.VMEM)
SM = pl.BlockSpec(memory_space=pltpu.SMEM)


def shape(*dims):
    return jax.ShapeDtypeStruct(dims, jnp.float32)


def call(kernel, outs, ins, args, scratch=(), room=32 * 1024):
    return pl.pallas_call(
        kernel,
        out_shape=outs,
        in_specs=ins,
        out_specs=jax.tree.map(lambda _: VM, outs),
        scratch_shapes=scratch,
        compiler_params=pltpu.CompilerParams(vmem_limit_bytes=room * 1024),
    )(*args)


def over_slab(value):
    return (value * 43691) >> 23


def coordinates():
    me = lax.axis_index("all")
    y = over_slab(2 * me)
    rest = me - y * (NX * NZ * NC)
    return y, rest >> 1, rest & 1


def device(y, x, z, c):
    return ((y * NX + x) * NZ + z) * NC + c


PAIRS = [[device(y, x, z, 0), device(y, x, z, 1)] for y in range(NY) for x in range(NX) for z in range(NZ)]
LINES = [
    [device(y, x, z, c) for x in pair for z in range(NZ)]
    for y in range(NY)
    for pair in ((0, 1), (3, 2))
    for c in range(NC)
]
PLANES = [
    [device(y, x, z, c) for x in pair for y in range(NY)]
    for z in range(NZ)
    for pair in ((0, 3), (1, 2))
    for c in range(NC)
]
CHIPS_Z = [
    [device(y, x, z, c) for z in range(NZ) for c in range(NC)] for y in range(NY) for x in range(NX)
]
ALL_YX = [
    [device(y, x, z, c) for y in range(NY) for x in range(NX)] for z in range(NZ) for c in range(NC)
]


def swap(array, groups):
    return lax.all_to_all(array, "all", 0, 0, tiled=True, axis_index_groups=groups)


def placed(lists):
    rows, cols, count = lists
    y, _, _ = coordinates()
    places = []
    for k in range(TS):
        column = cols[0, k]
        region = over_slab(column)
        within = column - region * SLAB
        slot = jnp.clip(within >> 2, 0, TABLE - 1)
        at = jnp.clip(region - y + 1, 0, 2) * JB + (within & 3)
        weight = jnp.where(k < count[0], jnp.float32(1.0), jnp.float32(0.0))
        places.append((jnp.clip(rows[0, k], 0, RB - 1), slot, at, weight))
    return places


def picked(cells, slot, at):
    return cells[slot, at >> 2, pl.ds(at & 3, 1), :]


def own_rows(cells):
    _, slot, core = coordinates()
    return cells[slot, 1, pl.ds(core * 2, 2), :]


def total(value):
    return jnp.sum(jnp.sum(value, axis=0, keepdims=True), axis=1, keepdims=True)


def packed(values):
    lane = lax.broadcasted_iota(jnp.int32, (1, LANES), 1)
    row = jnp.zeros((1, LANES), jnp.float32)
    for i, value in enumerate(values):
        row = jnp.where(lane == i, value, row)
    return row


def backward_terms(places, tiles, columns, table):
    shift = 2 if table.shape[2] == JB else 1
    for k, (r, slot, at, weight) in enumerate(places):
        term = jnp.sum(tiles[k] * columns[r], axis=0, keepdims=True) * weight
        row = pl.ds(at & (table.shape[2] - 1), 1)
        table[slot, at >> shift, row, :] = table[slot, at >> shift, row, :] + term


def started(pairs, sems):
    moves = [pltpu.make_async_copy(src, dst, sems.at[i]) for i, (src, dst) in enumerate(pairs)]
    for move in moves:
        move.start()
    return moves


def first_kernel(rows_far, cols_far, count, tiles_far, times, table, times_t, columns, tiles, rows, cols, sems):
    moves = started([(tiles_far, tiles), (rows_far, rows), (cols_far, cols)], sems)
    padded = jnp.concatenate([times[...], jnp.zeros((LANES - RB, LANES), jnp.float32)], axis=0)
    turned = padded.T
    times_t[...] = turned
    for r in range(RB):
        columns[r] = jnp.broadcast_to(turned[:, r : r + 1], (LANES, LANES))
    table[...] = jnp.zeros_like(table)
    moves[1].wait()
    moves[2].wait()
    places = placed((rows, cols, count))
    moves[0].wait()
    backward_terms(places, tiles, columns, table)


def second_kernel(rows_far, cols_far, count, tiles, cells, times_t, table, image_t, columns, rows, cols, sems):
    moves = started([(rows_far, rows), (cols_far, cols)], sems)
    columns[...] = jnp.zeros_like(columns)
    table[...] = jnp.zeros_like(table)
    moves[0].wait()
    moves[1].wait()
    places = placed((rows, cols, count))
    for k, (r, slot, at, weight) in enumerate(places):
        term = jnp.sum(tiles[k] * picked(cells, slot, at), axis=1, keepdims=True) * weight
        columns[r] = columns[r] + term
    lane = lax.broadcasted_iota(jnp.int32, (LANES, LANES), 1)
    image = jnp.zeros((LANES, LANES), jnp.float32)
    for r in range(RB):
        image = jnp.where(lane == r, columns[r], image)
    image_t[...] = image
    times = times_t[...]
    own = own_rows(cells)
    row = packed([total(times * times), total(own * own), total(image * image), total(image * times)])
    row = jnp.broadcast_to(row, (2, LANES))
    for s in range(TABLE):
        table[s, SLOT // 2] = row
    backward_terms(places, tiles, columns, table)


def third_kernel(rows, cols, count, tiles, cells, cells_2, times_t, image_t, sums, copies, held):
    times_sum, cells_sum, image_sum, cross = (sums[:, i : i + 1] for i in range(4))
    beta_1 = jnp.sqrt(times_sum)
    square = cells_sum / times_sum
    alpha_1 = jnp.sqrt(square)
    beta_2 = jnp.sqrt(image_sum / cells_sum - 2.0 * (cross / times_sum) + square)
    scale = 1.0 / (beta_1 * alpha_1 * beta_2)
    shift = (alpha_1 / beta_2 + beta_2 / alpha_1) / beta_1
    lane = lax.broadcasted_iota(jnp.int32, (LANES, LANES), 1)
    image_2 = jnp.zeros((LANES, LANES), jnp.float32)
    for k, (r, slot, at, weight) in enumerate(placed((rows, cols, count))):
        term = jnp.sum(tiles[k] * picked(cells_2, slot, at), axis=1, keepdims=True) * weight
        image_2 = image_2 + jnp.where(lane == r, term, 0.0)
    image = scale * image_2 - shift * image_t[...]
    ray = (image_t[...] / (alpha_1 * beta_1) - (alpha_1 / beta_1) * times_t[...]) / beta_2
    own_1 = own_rows(cells)
    own_2 = scale * own_rows(cells_2) - shift * own_1
    row = packed([total(own_2 * own_2), total(image * image), total(image * ray)])
    copies[...] = jnp.broadcast_to(row[None], copies.shape)
    rho_1 = jnp.sqrt(alpha_1 * alpha_1 + beta_2 * beta_2)
    cosine, sine = alpha_1 / rho_1, beta_2 / rho_1
    direction = own_1 / (beta_1 * alpha_1)
    held[0] = own_2
    held[1] = (cosine * beta_1 / rho_1) * direction
    held[2] = (sine / rho_1) * direction
    for i, value in enumerate([cosine, sine, sine * beta_1]):
        held[3 + i] = jnp.broadcast_to(value, (2, LANES))


def last_kernel(rows, held, update, ratio):
    cells_sum, image_sum, cross = (jnp.sum(rows[:, :, i : i + 1], axis=0) for i in range(3))
    alpha_2 = jnp.sqrt(cells_sum)
    beta_3 = jnp.sqrt(image_sum / cells_sum - 2.0 * cross + cells_sum)
    direction = held[0] / alpha_2 - alpha_2 * held[2]
    rho_bar = -held[3] * alpha_2
    rho_2 = jnp.sqrt(rho_bar * rho_bar + beta_3 * beta_3)
    update[...] = held[1] + (rho_bar / rho_2 * held[5] / rho_2) * direction
    ratio[...] = (beta_3 / rho_2[0:1, 0:1]) * held[4][0:1, 0:1]


def line_kernel(parts, copies):
    part = parts[0]
    for s in range(1, SLOTS):
        part = part + parts[s]
    for s in range(NY * NH):
        copies[s] = part


def plane_kernel(parts, copies, *sums):
    y, _, _ = coordinates()
    width = parts.shape[2]
    for d in range(3):
        for i in range(JB // width):
            acc = jnp.zeros((width, LANES), jnp.float32)
            for e in range(3):
                other = y + (d + e - 2)
                inside = jnp.logical_and(other >= 0, other < NY)
                other = jnp.clip(other, 0, NY - 1)
                at = (2 - e) * (JB // width) + i
                acc = acc + jnp.where(inside, parts[other, at] + parts[other + NY, at], 0.0)
            for s in range(SLOTS):
                copies[s, d, i * width : (i + 1) * width, :] = acc
    if sums:
        row = parts[0, SLOT // 2]
        for s in range(1, NY * NH):
            row = row + parts[s, SLOT // 2]
        sums[0][...] = row[0:1, :]


def exchange(table):
    _, _, core = coordinates()
    slot = table.shape[1:]
    pair = lax.all_gather(table.reshape((NC, SLOTS) + slot), "all", axis=0, axis_index_groups=PAIRS)
    half = lax.dynamic_index_in_dim(pair, core, axis=1, keepdims=False).sum(0)
    copies = call(line_kernel, shape(NY * NH, *slot), [VM], (swap(half, LINES),))
    outs = [shape(SLOTS, *NARROW, LANES)] + [shape(1, LANES)] * (slot[1] != JB)
    copies, *sums = call(plane_kernel, outs, [VM], (swap(copies, PLANES),))
    full = lax.all_gather(swap(copies, LINES), "all", axis=0, axis_index_groups=PAIRS)
    return full.reshape(TABLE, *NARROW, LANES), *sums


def local(sensitivity, tile_rows, tile_cols, tile_count, travel_times):
    tiles = sensitivity[0]
    lists = (tile_rows, tile_cols, tile_count)
    square = shape(LANES, LANES)
    columns = pltpu.VMEM((RB, LANES, LANES), jnp.float32)
    far = pl.BlockSpec(memory_space=pl.ANY)
    short = [pltpu.SMEM((1, TS), jnp.int32)] * 2

    table, times_t = call(
        first_kernel,
        [shape(TABLE, *NARROW, LANES), square],
        [far, far, SM, far, VM],
        (*lists, tiles, travel_times),
        [columns, columns, *short, pltpu.SemaphoreType.DMA((3,))],
        54528,
    )
    (cells,) = exchange(table)
    table, image_t = call(
        second_kernel,
        [shape(TABLE, *PAIRED, LANES), square],
        [far, far, SM] + [VM] * 3,
        (*lists, tiles, cells, times_t),
        [columns, *short, pltpu.SemaphoreType.DMA((2,))],
    )
    cells_2, sums = exchange(table)
    copies, held = call(
        third_kernel,
        [shape(NZ * NC, 1, LANES), shape(6, 2, LANES)],
        [SM] * 3 + [VM] * 6,
        (*lists, tiles, cells, cells_2, times_t, image_t, sums),
    )
    rows = swap(copies, CHIPS_Z).sum(0)
    rows = swap(jnp.broadcast_to(rows[None], (NY * NX, 1, LANES)), ALL_YX)
    update, ratio = call(last_kernel, [shape(2, LANES), shape(1, 1)], [VM] * 2, (rows, held))
    return update, ratio.reshape(1)


def solution(mesh):
    flat = Mesh(mesh.devices.reshape(-1), ("all",))
    every = P("all")
    return jax.shard_map(
        local, mesh=flat, in_specs=(every,) * 5, out_specs=(every, P()), check_vma=False
    )
```

```python
import jax
import jax.numpy as jnp
from jax import lax
from jax.experimental import pallas as pl
from jax.experimental.pallas import tpu as pltpu
from jax.sharding import Mesh, PartitionSpec as P

NY, NX, NZ, NC = 8, 4, 12, 2
NH = 2
SLAB = 192
SLOTS = NH * NZ
JB = SLAB // (NC * SLOTS)
SLOT = 3 * JB
NARROW = (3, JB)
PAIRED = (SLOT // 2 + 1, 2)
LANES = 128
TABLE = NC * SLOTS
TS = 16
RB = 16
VM = pl.BlockSpec(memory_space=pltpu.VMEM)
SM = pl.BlockSpec(memory_space=pltpu.SMEM)


def shape(*dims):
    return jax.ShapeDtypeStruct(dims, jnp.float32)


def call(kernel, outs, ins, args, scratch=(), room=32 * 1024):
    return pl.pallas_call(
        kernel,
        out_shape=outs,
        in_specs=ins,
        out_specs=jax.tree.map(lambda _: VM, outs),
        scratch_shapes=scratch,
        compiler_params=pltpu.CompilerParams(vmem_limit_bytes=room * 1024),
    )(*args)


def over_slab(value):
    return (value * 43691) >> 23


def coordinates():
    me = lax.axis_index("all")
    y = over_slab(2 * me)
    rest = me - y * (NX * NZ * NC)
    return y, rest >> 1, rest & 1


def device(y, x, z, c):
    return ((y * NX + x) * NZ + z) * NC + c


PAIRS = [[device(y, x, z, 0), device(y, x, z, 1)] for y in range(NY) for x in range(NX) for z in range(NZ)]
LINES = [
    [device(y, x, z, c) for z in range(NZ) for x in pair]
    for y in range(NY)
    for pair in ((0, 1), (3, 2))
    for c in range(NC)
]
PLANES = [
    [device(y, x, z, c) for x in pair for y in range(NY)]
    for z in range(NZ)
    for pair in ((0, 3), (1, 2))
    for c in range(NC)
]
CHIPS_Z = [
    [device(y, x, z, c) for z in range(NZ) for c in range(NC)] for y in range(NY) for x in range(NX)
]
ALL_YX = [
    [device(y, x, z, c) for y in range(NY) for x in range(NX)] for z in range(NZ) for c in range(NC)
]


def swap(array, groups):
    return lax.all_to_all(array, "all", 0, 0, tiled=True, axis_index_groups=groups)


def placed(lists):
    rows, cols, count = lists
    y, _, _ = coordinates()
    places = []
    for k in range(TS):
        column = cols[0, k]
        region = over_slab(column)
        within = column - region * SLAB
        slot = jnp.clip(within >> 2, 0, TABLE - 1)
        at = jnp.clip(region - y + 1, 0, 2) * JB + (within & 3)
        weight = jnp.where(k < count[0], jnp.float32(1.0), jnp.float32(0.0))
        places.append((jnp.clip(rows[0, k], 0, RB - 1), slot, at, weight))
    return places


def picked(cells, slot, at):
    return cells[slot, at >> 2, pl.ds(at & 3, 1), :]


def own_rows(cells):
    _, slot, core = coordinates()
    return cells[slot, 1, pl.ds(core * 2, 2), :]


def total(value):
    return jnp.sum(jnp.sum(value, axis=0, keepdims=True), axis=1, keepdims=True)


def packed(values):
    lane = lax.broadcasted_iota(jnp.int32, (1, LANES), 1)
    row = jnp.zeros((1, LANES), jnp.float32)
    for i, value in enumerate(values):
        row = jnp.where(lane == i, value, row)
    return row


def backward_terms(places, tiles, columns, table):
    shift = 2 if table.shape[2] == JB else 1
    for k, (r, slot, at, weight) in enumerate(places):
        term = jnp.sum(tiles[k] * columns[r], axis=0, keepdims=True) * weight
        row = pl.ds(at & (table.shape[2] - 1), 1)
        table[slot, at >> shift, row, :] = table[slot, at >> shift, row, :] + term


def started(pairs, sems):
    moves = [pltpu.make_async_copy(src, dst, sems.at[i]) for i, (src, dst) in enumerate(pairs)]
    for move in moves:
        move.start()
    return moves


def first_kernel(rows_far, cols_far, count, tiles_far, times, table, times_t, columns, tiles, rows, cols, sems):
    moves = started([(tiles_far, tiles), (rows_far, rows), (cols_far, cols)], sems)
    padded = jnp.concatenate([times[...], jnp.zeros((LANES - RB, LANES), jnp.float32)], axis=0)
    turned = padded.T
    times_t[...] = turned
    for r in range(RB):
        columns[r] = jnp.broadcast_to(turned[:, r : r + 1], (LANES, LANES))
    table[...] = jnp.zeros_like(table)
    moves[1].wait()
    moves[2].wait()
    places = placed((rows, cols, count))
    moves[0].wait()
    backward_terms(places, tiles, columns, table)


def second_kernel(rows_far, cols_far, count, tiles, cells, times_t, table, image_t, columns, rows, cols, sems):
    moves = started([(rows_far, rows), (cols_far, cols)], sems)
    columns[...] = jnp.zeros_like(columns)
    table[...] = jnp.zeros_like(table)
    moves[0].wait()
    moves[1].wait()
    places = placed((rows, cols, count))
    for k, (r, slot, at, weight) in enumerate(places):
        term = jnp.sum(tiles[k] * picked(cells, slot, at), axis=1, keepdims=True) * weight
        columns[r] = columns[r] + term
    lane = lax.broadcasted_iota(jnp.int32, (LANES, LANES), 1)
    image = jnp.zeros((LANES, LANES), jnp.float32)
    for r in range(RB):
        image = jnp.where(lane == r, columns[r], image)
    image_t[...] = image
    times = times_t[...]
    own = own_rows(cells)
    row = packed([total(times * times), total(own * own), total(image * image), total(image * times)])
    row = jnp.broadcast_to(row, (2, LANES))
    for s in range(TABLE):
        table[s, SLOT // 2] = row
    backward_terms(places, tiles, columns, table)


def third_kernel(rows, cols, count, tiles, cells, cells_2, times_t, image_t, sums, copies, held):
    times_sum, cells_sum, image_sum, cross = (sums[:, i : i + 1] for i in range(4))
    beta_1 = jnp.sqrt(times_sum)
    square = cells_sum / times_sum
    alpha_1 = jnp.sqrt(square)
    beta_2 = jnp.sqrt(image_sum / cells_sum - 2.0 * (cross / times_sum) + square)
    scale = 1.0 / (beta_1 * alpha_1 * beta_2)
    shift = (alpha_1 / beta_2 + beta_2 / alpha_1) / beta_1
    lane = lax.broadcasted_iota(jnp.int32, (LANES, LANES), 1)
    image_2 = jnp.zeros((LANES, LANES), jnp.float32)
    for k, (r, slot, at, weight) in enumerate(placed((rows, cols, count))):
        term = jnp.sum(tiles[k] * picked(cells_2, slot, at), axis=1, keepdims=True) * weight
        image_2 = image_2 + jnp.where(lane == r, term, 0.0)
    image = scale * image_2 - shift * image_t[...]
    ray = (image_t[...] / (alpha_1 * beta_1) - (alpha_1 / beta_1) * times_t[...]) / beta_2
    own_1 = own_rows(cells)
    own_2 = scale * own_rows(cells_2) - shift * own_1
    row = packed([total(own_2 * own_2), total(image * image), total(image * ray)])
    copies[...] = jnp.broadcast_to(row[None], copies.shape)
    rho_1 = jnp.sqrt(alpha_1 * alpha_1 + beta_2 * beta_2)
    cosine, sine = alpha_1 / rho_1, beta_2 / rho_1
    direction = own_1 / (beta_1 * alpha_1)
    held[0] = own_2
    held[1] = (cosine * beta_1 / rho_1) * direction
    held[2] = (sine / rho_1) * direction
    for i, value in enumerate([cosine, sine, sine * beta_1]):
        held[3 + i] = jnp.broadcast_to(value, (2, LANES))


def last_kernel(rows, held, update, ratio):
    cells_sum, image_sum, cross = (jnp.sum(rows[:, :, i : i + 1], axis=0) for i in range(3))
    alpha_2 = jnp.sqrt(cells_sum)
    beta_3 = jnp.sqrt(image_sum / cells_sum - 2.0 * cross + cells_sum)
    direction = held[0] / alpha_2 - alpha_2 * held[2]
    rho_bar = -held[3] * alpha_2
    rho_2 = jnp.sqrt(rho_bar * rho_bar + beta_3 * beta_3)
    update[...] = held[1] + (rho_bar / rho_2 * held[5] / rho_2) * direction
    ratio[...] = (beta_3 / rho_2[0:1, 0:1]) * held[4][0:1, 0:1]


def line_kernel(parts, copies):
    part = parts[0]
    for s in range(1, SLOTS):
        part = part + parts[s]
    for s in range(NY * NH):
        copies[s] = part


def plane_kernel(parts, copies, *sums):
    y, _, _ = coordinates()
    width = parts.shape[2]
    for d in range(3):
        for i in range(JB // width):
            acc = jnp.zeros((width, LANES), jnp.float32)
            for e in range(3):
                other = y + (d + e - 2)
                inside = jnp.logical_and(other >= 0, other < NY)
                other = jnp.clip(other, 0, NY - 1)
                at = (2 - e) * (JB // width) + i
                acc = acc + jnp.where(inside, parts[other, at] + parts[other + NY, at], 0.0)
            for s in range(SLOTS):
                copies[s, d, i * width : (i + 1) * width, :] = acc
    if sums:
        row = parts[0, SLOT // 2]
        for s in range(1, NY * NH):
            row = row + parts[s, SLOT // 2]
        sums[0][...] = row[0:1, :]


def exchange(table):
    _, _, core = coordinates()
    slot = table.shape[1:]
    pair = lax.all_gather(table.reshape((NC, SLOTS) + slot), "all", axis=0, axis_index_groups=PAIRS)
    half = lax.dynamic_index_in_dim(pair, core, axis=1, keepdims=False).sum(0)
    copies = call(line_kernel, shape(NY * NH, *slot), [VM], (swap(half, LINES),))
    outs = [shape(SLOTS, *NARROW, LANES)] + [shape(1, LANES)] * (slot[1] != JB)
    copies, *sums = call(plane_kernel, outs, [VM], (swap(copies, PLANES),))
    full = lax.all_gather(swap(copies, LINES), "all", axis=0, axis_index_groups=PAIRS)
    return full.reshape(TABLE, *NARROW, LANES), *sums


def local(sensitivity, tile_rows, tile_cols, tile_count, travel_times):
    tiles = sensitivity[0]
    lists = (tile_rows, tile_cols, tile_count)
    square = shape(LANES, LANES)
    columns = pltpu.VMEM((RB, LANES, LANES), jnp.float32)
    far = pl.BlockSpec(memory_space=pl.ANY)
    short = [pltpu.SMEM((1, TS), jnp.int32)] * 2

    table, times_t = call(
        first_kernel,
        [shape(TABLE, *NARROW, LANES), square],
        [far, far, SM, far, VM],
        (*lists, tiles, travel_times),
        [columns, columns, *short, pltpu.SemaphoreType.DMA((3,))],
        54528,
    )
    (cells,) = exchange(table)
    table, image_t = call(
        second_kernel,
        [shape(TABLE, *PAIRED, LANES), square],
        [far, far, SM] + [VM] * 3,
        (*lists, tiles, cells, times_t),
        [columns, *short, pltpu.SemaphoreType.DMA((2,))],
    )
    cells_2, sums = exchange(table)
    copies, held = call(
        third_kernel,
        [shape(NZ * NC, 1, LANES), shape(6, 2, LANES)],
        [SM] * 3 + [VM] * 6,
        (*lists, tiles, cells, cells_2, times_t, image_t, sums),
    )
    rows = swap(copies, CHIPS_Z).sum(0)
    rows = swap(jnp.broadcast_to(rows[None], (NY * NX, 1, LANES)), ALL_YX)
    update, ratio = call(last_kernel, [shape(2, LANES), shape(1, 1)], [VM] * 2, (rows, held))
    return update, ratio.reshape(1)


def solution(mesh):
    flat = Mesh(mesh.devices.reshape(-1), ("all",))
    every = P("all")
    return jax.shard_map(
        local, mesh=flat, in_specs=(every,) * 5, out_specs=(every, P()), check_vma=False
    )
```

```python
import jax
import jax.numpy as jnp
from jax import lax
from jax.experimental import pallas as pl
from jax.experimental.pallas import tpu as pltpu
from jax.sharding import Mesh, PartitionSpec as P

NY, NX, NZ, NC = 8, 4, 12, 2
NH = 2
SLAB = 192
SLOTS = NH * NZ
JB = SLAB // (NC * SLOTS)
SLOT = 3 * JB
NARROW = (3, JB)
PAIRED = (SLOT // 2 + 1, 2)
LANES = 128
TABLE = NC * SLOTS
TS = 16
RB = 16
VM = pl.BlockSpec(memory_space=pltpu.VMEM)
SM = pl.BlockSpec(memory_space=pltpu.SMEM)


def shape(*dims):
    return jax.ShapeDtypeStruct(dims, jnp.float32)


def call(kernel, outs, ins, args, scratch=(), room=32 * 1024):
    return pl.pallas_call(
        kernel,
        out_shape=outs,
        in_specs=ins,
        out_specs=jax.tree.map(lambda _: VM, outs),
        scratch_shapes=scratch,
        compiler_params=pltpu.CompilerParams(vmem_limit_bytes=room * 1024),
    )(*args)


def over_slab(value):
    return (value * 43691) >> 23


def coordinates():
    me = lax.axis_index("all")
    y = over_slab(2 * me)
    rest = me - y * (NX * NZ * NC)
    return y, rest >> 1, rest & 1


def device(y, x, z, c):
    return ((y * NX + x) * NZ + z) * NC + c


PAIRS = [[device(y, x, z, 0), device(y, x, z, 1)] for y in range(NY) for x in range(NX) for z in range(NZ)]
LINES = [
    [device(y, x, z, c) for z in range(NZ) for x in pair]
    for y in range(NY)
    for pair in ((0, 1), (3, 2))
    for c in range(NC)
]
PLANES = [
    [device(y, x, z, c) for x in pair for y in range(NY)]
    for z in range(NZ)
    for pair in ((0, 3), (1, 2))
    for c in range(NC)
]
CHIPS_Z = [
    [device(y, x, z, c) for z in range(NZ) for c in range(NC)] for y in range(NY) for x in range(NX)
]
ALL_YX = [
    [device(y, x, z, c) for y in range(NY) for x in range(NX)] for z in range(NZ) for c in range(NC)
]


def swap(array, groups):
    return lax.all_to_all(array, "all", 0, 0, tiled=True, axis_index_groups=groups)


def placed(lists):
    rows, cols, count = lists
    y, _, _ = coordinates()
    places = []
    for k in range(TS):
        column = cols[0, k]
        region = over_slab(column)
        within = column - region * SLAB
        slot = jnp.clip(within >> 2, 0, TABLE - 1)
        at = jnp.clip(region - y + 1, 0, 2) * JB + (within & 3)
        weight = jnp.where(k < count[0], jnp.float32(1.0), jnp.float32(0.0))
        places.append((jnp.clip(rows[0, k], 0, RB - 1), slot, at, weight))
    return places


def picked(cells, slot, at):
    return cells[slot, at >> 2, pl.ds(at & 3, 1), :]


def own_rows(cells):
    _, slot, core = coordinates()
    return cells[slot, 1, pl.ds(core * 2, 2), :]


def total(value):
    return jnp.sum(jnp.sum(value, axis=0, keepdims=True), axis=1, keepdims=True)


def packed(values):
    lane = lax.broadcasted_iota(jnp.int32, (1, LANES), 1)
    row = jnp.zeros((1, LANES), jnp.float32)
    for i, value in enumerate(values):
        row = jnp.where(lane == i, value, row)
    return row


def backward_terms(places, tiles, columns, table, first=0, end=TS):
    shift = 2 if table.shape[2] == JB else 1
    for k in range(first, end):
        r, slot, at, weight = places[k]
        term = jnp.sum(tiles[k] * columns[r], axis=0, keepdims=True) * weight
        row = pl.ds(at & (table.shape[2] - 1), 1)
        table[slot, at >> shift, row, :] = table[slot, at >> shift, row, :] + term


def started(pairs, sems):
    moves = [pltpu.make_async_copy(src, dst, sems.at[i]) for i, (src, dst) in enumerate(pairs)]
    for move in moves:
        move.start()
    return moves


def first_kernel(rows_far, cols_far, count, tiles_far, times, table, times_t, columns, tiles, rows, cols, sems):
    parts = [pl.ds(k, TS // 4) for k in range(0, TS, TS // 4)]
    pairs = [(rows_far, rows), (cols_far, cols)] + [(tiles_far.at[p], tiles.at[p]) for p in parts]
    moves = started(pairs, sems)
    padded = jnp.concatenate([times[...], jnp.zeros((LANES - RB, LANES), jnp.float32)], axis=0)
    turned = padded.T
    times_t[...] = turned
    for r in range(RB):
        columns[r] = jnp.broadcast_to(turned[:, r : r + 1], (LANES, LANES))
    table[...] = jnp.zeros_like(table)
    moves[0].wait()
    moves[1].wait()
    places = placed((rows, cols, count))
    for i, move in enumerate(moves[2:]):
        move.wait()
        backward_terms(places, tiles, columns, table, i * TS // 4, (i + 1) * TS // 4)


def second_kernel(rows_far, cols_far, count, tiles, cells, times_t, table, image_t, columns, rows, cols, sems):
    moves = started([(rows_far, rows), (cols_far, cols)], sems)
    columns[...] = jnp.zeros_like(columns)
    table[...] = jnp.zeros_like(table)
    moves[0].wait()
    moves[1].wait()
    places = placed((rows, cols, count))
    for k, (r, slot, at, weight) in enumerate(places):
        term = jnp.sum(tiles[k] * picked(cells, slot, at), axis=1, keepdims=True) * weight
        columns[r] = columns[r] + term
    lane = lax.broadcasted_iota(jnp.int32, (LANES, LANES), 1)
    image = jnp.zeros((LANES, LANES), jnp.float32)
    for r in range(RB):
        image = jnp.where(lane == r, columns[r], image)
    image_t[...] = image
    times = times_t[...]
    own = own_rows(cells)
    row = packed([total(times * times), total(own * own), total(image * image), total(image * times)])
    row = jnp.broadcast_to(row, (2, LANES))
    for s in range(TABLE):
        table[s, SLOT // 2] = row
    backward_terms(places, tiles, columns, table)


def third_kernel(rows, cols, count, tiles, cells, cells_2, times_t, image_t, sums, copies, held):
    times_sum, cells_sum, image_sum, cross = (sums[:, i : i + 1] for i in range(4))
    beta_1 = jnp.sqrt(times_sum)
    square = cells_sum / times_sum
    alpha_1 = jnp.sqrt(square)
    beta_2 = jnp.sqrt(image_sum / cells_sum - 2.0 * (cross / times_sum) + square)
    scale = 1.0 / (beta_1 * alpha_1 * beta_2)
    shift = (alpha_1 / beta_2 + beta_2 / alpha_1) / beta_1
    lane = lax.broadcasted_iota(jnp.int32, (LANES, LANES), 1)
    image_2 = jnp.zeros((LANES, LANES), jnp.float32)
    for k, (r, slot, at, weight) in enumerate(placed((rows, cols, count))):
        term = jnp.sum(tiles[k] * picked(cells_2, slot, at), axis=1, keepdims=True) * weight
        image_2 = image_2 + jnp.where(lane == r, term, 0.0)
    image = scale * image_2 - shift * image_t[...]
    ray = (image_t[...] / (alpha_1 * beta_1) - (alpha_1 / beta_1) * times_t[...]) / beta_2
    own_1 = own_rows(cells)
    own_2 = scale * own_rows(cells_2) - shift * own_1
    row = packed([total(own_2 * own_2), total(image * image), total(image * ray)])
    copies[...] = jnp.broadcast_to(row[None], copies.shape)
    rho_1 = jnp.sqrt(alpha_1 * alpha_1 + beta_2 * beta_2)
    cosine, sine = alpha_1 / rho_1, beta_2 / rho_1
    direction = own_1 / (beta_1 * alpha_1)
    held[0] = own_2
    held[1] = (cosine * beta_1 / rho_1) * direction
    held[2] = (sine / rho_1) * direction
    for i, value in enumerate([cosine, sine, sine * beta_1]):
        held[3 + i] = jnp.broadcast_to(value, (2, LANES))


def last_kernel(rows, held, update, ratio):
    cells_sum, image_sum, cross = (jnp.sum(rows[:, :, i : i + 1], axis=0) for i in range(3))
    alpha_2 = jnp.sqrt(cells_sum)
    beta_3 = jnp.sqrt(image_sum / cells_sum - 2.0 * cross + cells_sum)
    direction = held[0] / alpha_2 - alpha_2 * held[2]
    rho_bar = -held[3] * alpha_2
    rho_2 = jnp.sqrt(rho_bar * rho_bar + beta_3 * beta_3)
    update[...] = held[1] + (rho_bar / rho_2 * held[5] / rho_2) * direction
    ratio[...] = (beta_3 / rho_2[0:1, 0:1]) * held[4][0:1, 0:1]


def line_kernel(parts, copies):
    part = parts[0]
    for s in range(1, SLOTS):
        part = part + parts[s]
    for s in range(NY * NH):
        copies[s] = part


def plane_kernel(parts, copies, *sums):
    y, _, _ = coordinates()
    width = parts.shape[2]
    for d in range(3):
        for i in range(JB // width):
            acc = jnp.zeros((width, LANES), jnp.float32)
            for e in range(3):
                other = y + (d + e - 2)
                inside = jnp.logical_and(other >= 0, other < NY)
                other = jnp.clip(other, 0, NY - 1)
                at = (2 - e) * (JB // width) + i
                acc = acc + jnp.where(inside, parts[other, at] + parts[other + NY, at], 0.0)
            for s in range(SLOTS):
                copies[s, d, i * width : (i + 1) * width, :] = acc
    if sums:
        row = parts[0, SLOT // 2]
        for s in range(1, NY * NH):
            row = row + parts[s, SLOT // 2]
        sums[0][...] = row[0:1, :]


def exchange(table):
    _, _, core = coordinates()
    slot = table.shape[1:]
    pair = lax.all_gather(table.reshape((NC, SLOTS) + slot), "all", axis=0, axis_index_groups=PAIRS)
    half = lax.dynamic_index_in_dim(pair, core, axis=1, keepdims=False).sum(0)
    copies = call(line_kernel, shape(NY * NH, *slot), [VM], (swap(half, LINES),))
    outs = [shape(SLOTS, *NARROW, LANES)] + [shape(1, LANES)] * (slot[1] != JB)
    copies, *sums = call(plane_kernel, outs, [VM], (swap(copies, PLANES),))
    full = lax.all_gather(swap(copies, LINES), "all", axis=0, axis_index_groups=PAIRS)
    return full.reshape(TABLE, *NARROW, LANES), *sums


def local(sensitivity, tile_rows, tile_cols, tile_count, travel_times):
    tiles = sensitivity[0]
    lists = (tile_rows, tile_cols, tile_count)
    square = shape(LANES, LANES)
    columns = pltpu.VMEM((RB, LANES, LANES), jnp.float32)
    far = pl.BlockSpec(memory_space=pl.ANY)
    short = [pltpu.SMEM((1, TS), jnp.int32)] * 2

    table, times_t = call(
        first_kernel,
        [shape(TABLE, *NARROW, LANES), square],
        [far, far, SM, far, VM],
        (*lists, tiles, travel_times),
        [columns, columns, *short, pltpu.SemaphoreType.DMA((6,))],
        54528,
    )
    (cells,) = exchange(table)
    table, image_t = call(
        second_kernel,
        [shape(TABLE, *PAIRED, LANES), square],
        [far, far, SM] + [VM] * 3,
        (*lists, tiles, cells, times_t),
        [columns, *short, pltpu.SemaphoreType.DMA((2,))],
    )
    cells_2, sums = exchange(table)
    copies, held = call(
        third_kernel,
        [shape(NZ * NC, 1, LANES), shape(6, 2, LANES)],
        [SM] * 3 + [VM] * 6,
        (*lists, tiles, cells, cells_2, times_t, image_t, sums),
    )
    rows = swap(copies, CHIPS_Z).sum(0)
    rows = swap(jnp.broadcast_to(rows[None], (NY * NX, 1, LANES)), ALL_YX)
    update, ratio = call(last_kernel, [shape(2, LANES), shape(1, 1)], [VM] * 2, (rows, held))
    return update, ratio.reshape(1)


def solution(mesh):
    flat = Mesh(mesh.devices.reshape(-1), ("all",))
    every = P("all")
    return jax.shard_map(
        local, mesh=flat, in_specs=(every,) * 5, out_specs=(every, P()), check_vma=False
    )
```

```python
import jax
import jax.numpy as jnp
from jax import lax
from jax.experimental import pallas as pl
from jax.experimental.pallas import tpu as pltpu
from jax.sharding import Mesh, PartitionSpec as P

NY, NX, NZ, NC = 8, 4, 12, 2
NH = 2
SLAB = 192
SLOTS = NH * NZ
JB = SLAB // (NC * SLOTS)
SLOT = 3 * JB
NARROW = (3, JB)
PAIRED = (SLOT // 2 + 1, 2)
LANES = 128
TABLE = NC * SLOTS
TS = 16
RB = 16
VM = pl.BlockSpec(memory_space=pltpu.VMEM)
SM = pl.BlockSpec(memory_space=pltpu.SMEM)


def shape(*dims):
    return jax.ShapeDtypeStruct(dims, jnp.float32)


def call(kernel, outs, ins, args, scratch=(), room=32 * 1024):
    return pl.pallas_call(
        kernel,
        out_shape=outs,
        in_specs=ins,
        out_specs=jax.tree.map(lambda _: VM, outs),
        scratch_shapes=scratch,
        compiler_params=pltpu.CompilerParams(vmem_limit_bytes=room * 1024),
    )(*args)


def over_slab(value):
    return (value * 43691) >> 23


def coordinates():
    me = lax.axis_index("all")
    y = over_slab(2 * me)
    rest = me - y * (NX * NZ * NC)
    return y, rest >> 1, rest & 1


def device(y, x, z, c):
    return ((y * NX + x) * NZ + z) * NC + c


PAIRS = [[device(y, x, z, 0), device(y, x, z, 1)] for y in range(NY) for x in range(NX) for z in range(NZ)]
LINES = [
    [device(y, x, z, c) for z in range(NZ) for x in pair]
    for y in range(NY)
    for pair in ((0, 1), (3, 2))
    for c in range(NC)
]
PLANES = [
    [device(y, x, z, c) for x in pair for y in range(NY)]
    for z in range(NZ)
    for pair in ((0, 3), (1, 2))
    for c in range(NC)
]
CHIPS_Z = [
    [device(y, x, z, c) for z in range(NZ) for c in range(NC)] for y in range(NY) for x in range(NX)
]
ALL_YX = [
    [device(y, x, z, c) for y in range(NY) for x in range(NX)] for z in range(NZ) for c in range(NC)
]


def swap(array, groups):
    return lax.all_to_all(array, "all", 0, 0, tiled=True, axis_index_groups=groups)


def placed(lists):
    rows, cols, count = lists
    y, _, _ = coordinates()
    places = []
    for k in range(TS):
        column = cols[0, k]
        region = over_slab(column)
        within = column - region * SLAB
        slot = jnp.clip(within >> 2, 0, TABLE - 1)
        at = jnp.clip(region - y + 1, 0, 2) * JB + (within & 3)
        weight = jnp.where(k < count[0], jnp.float32(1.0), jnp.float32(0.0))
        places.append((jnp.clip(rows[0, k], 0, RB - 1), slot, at, weight))
    return places


def picked(cells, slot, at):
    return cells[slot, at >> 2, pl.ds(at & 3, 1), :]


def own_rows(cells):
    _, slot, core = coordinates()
    return cells[slot, 1, pl.ds(core * 2, 2), :]


def total(value):
    return jnp.sum(jnp.sum(value, axis=0, keepdims=True), axis=1, keepdims=True)


def packed(values):
    lane = lax.broadcasted_iota(jnp.int32, (1, LANES), 1)
    row = jnp.zeros((1, LANES), jnp.float32)
    for i, value in enumerate(values):
        row = jnp.where(lane == i, value, row)
    return row


def backward_terms(places, tiles, columns, table, first=0, end=TS):
    shift = 2 if table.shape[2] == JB else 1
    for k in range(first, end):
        r, slot, at, weight = places[k]
        term = jnp.sum(tiles[k] * columns[r], axis=0, keepdims=True) * weight
        row = pl.ds(at & (table.shape[2] - 1), 1)
        table[slot, at >> shift, row, :] = table[slot, at >> shift, row, :] + term


def started(pairs, sems):
    moves = [pltpu.make_async_copy(src, dst, sems.at[i]) for i, (src, dst) in enumerate(pairs)]
    for move in moves:
        move.start()
    return moves


def first_kernel(rows_far, cols_far, count, tiles_far, times, table, times_t, columns, tiles, rows, cols, sems):
    parts = [pl.ds(k, TS // 4) for k in range(0, TS, TS // 4)]
    pairs = [(rows_far, rows), (cols_far, cols)] + [(tiles_far.at[p], tiles.at[p]) for p in parts]
    moves = started(pairs, sems)
    padded = jnp.concatenate([times[...], jnp.zeros((LANES - RB, LANES), jnp.float32)], axis=0)
    turned = padded.T
    times_t[...] = turned
    for r in range(RB):
        columns[r] = jnp.broadcast_to(turned[:, r : r + 1], (LANES, LANES))
    table[...] = jnp.zeros_like(table)
    moves[0].wait()
    moves[1].wait()
    places = placed((rows, cols, count))
    for i, move in enumerate(moves[2:]):
        move.wait()
        backward_terms(places, tiles, columns, table, i * TS // 4, (i + 1) * TS // 4)


def second_kernel(rows_far, cols_far, count, tiles, cells, times_t, table, image_t, columns, rows, cols, sems):
    moves = started([(rows_far, rows), (cols_far, cols)], sems)
    columns[...] = jnp.zeros_like(columns)
    table[...] = jnp.zeros_like(table)
    moves[0].wait()
    moves[1].wait()
    places = placed((rows, cols, count))
    for k, (r, slot, at, weight) in enumerate(places):
        term = jnp.sum(tiles[k] * picked(cells, slot, at), axis=1, keepdims=True) * weight
        columns[r] = columns[r] + term
    lane = lax.broadcasted_iota(jnp.int32, (LANES, LANES), 1)
    image = jnp.zeros((LANES, LANES), jnp.float32)
    for r in range(RB):
        image = jnp.where(lane == r, columns[r], image)
    image_t[...] = image
    times = times_t[...]
    own = own_rows(cells)
    row = packed([total(times * times), total(own * own), total(image * image), total(image * times)])
    row = jnp.broadcast_to(row, (2, LANES))
    for s in range(TABLE):
        table[s, SLOT // 2] = row
    backward_terms(places, tiles, columns, table)


def third_kernel(rows, cols, count, tiles, cells, cells_2, times_t, image_t, sums, copies, held):
    times_sum, cells_sum, image_sum, cross = (sums[:, i : i + 1] for i in range(4))
    beta_1 = jnp.sqrt(times_sum)
    square = cells_sum / times_sum
    alpha_1 = jnp.sqrt(square)
    beta_2 = jnp.sqrt(image_sum / cells_sum - 2.0 * (cross / times_sum) + square)
    scale = 1.0 / (beta_1 * alpha_1 * beta_2)
    shift = (alpha_1 / beta_2 + beta_2 / alpha_1) / beta_1
    lane = lax.broadcasted_iota(jnp.int32, (LANES, LANES), 1)
    image_2 = jnp.zeros((LANES, LANES), jnp.float32)
    for k, (r, slot, at, weight) in enumerate(placed((rows, cols, count))):
        term = jnp.sum(tiles[k] * picked(cells_2, slot, at), axis=1, keepdims=True) * weight
        image_2 = image_2 + jnp.where(lane == r, term, 0.0)
    image = scale * image_2 - shift * image_t[...]
    ray = (image_t[...] / (alpha_1 * beta_1) - (alpha_1 / beta_1) * times_t[...]) / beta_2
    own_1 = own_rows(cells)
    own_2 = scale * own_rows(cells_2) - shift * own_1
    row = packed([total(own_2 * own_2), total(image * image), total(image * ray)])
    copies[...] = jnp.broadcast_to(row[None], copies.shape)
    rho_1 = jnp.sqrt(alpha_1 * alpha_1 + beta_2 * beta_2)
    cosine, sine = alpha_1 / rho_1, beta_2 / rho_1
    direction = own_1 / (beta_1 * alpha_1)
    held[0] = own_2
    held[1] = (cosine * beta_1 / rho_1) * direction
    held[2] = (sine / rho_1) * direction
    for i, value in enumerate([cosine, sine, sine * beta_1]):
        held[3 + i] = jnp.broadcast_to(value, (2, LANES))


def last_kernel(rows, held, update, ratio):
    cells_sum, image_sum, cross = (jnp.sum(rows[:, :, i : i + 1], axis=0) for i in range(3))
    alpha_2 = jnp.sqrt(cells_sum)
    beta_3 = jnp.sqrt(image_sum / cells_sum - 2.0 * cross + cells_sum)
    direction = held[0] / alpha_2 - alpha_2 * held[2]
    rho_bar = -held[3] * alpha_2
    rho_2 = jnp.sqrt(rho_bar * rho_bar + beta_3 * beta_3)
    update[...] = held[1] + (rho_bar / rho_2 * held[5] / rho_2) * direction
    ratio[...] = (beta_3 / rho_2[0:1, 0:1]) * held[4][0:1, 0:1]


def line_kernel(parts, copies):
    part = parts[0]
    for s in range(1, SLOTS):
        part = part + parts[s]
    for s in range(NY * NH):
        copies[s] = part


def plane_kernel(parts, copies, *sums):
    y, _, _ = coordinates()
    width = parts.shape[2]
    for d in range(3):
        for i in range(JB // width):
            acc = jnp.zeros((width, LANES), jnp.float32)
            for e in range(3):
                other = y + (d + e - 2)
                inside = jnp.logical_and(other >= 0, other < NY)
                other = jnp.clip(other, 0, NY - 1)
                at = (2 - e) * (JB // width) + i
                acc = acc + jnp.where(inside, parts[other, at] + parts[other + NY, at], 0.0)
            for s in range(SLOTS):
                copies[s, d, i * width : (i + 1) * width, :] = acc
    if sums:
        row = parts[0, SLOT // 2]
        for s in range(1, NY * NH):
            row = row + parts[s, SLOT // 2]
        sums[0][...] = row[0:1, :]


def exchange(table):
    _, _, core = coordinates()
    slot = table.shape[1:]
    pair = lax.all_gather(table.reshape((NC, SLOTS) + slot), "all", axis=0, axis_index_groups=PAIRS)
    half = lax.dynamic_index_in_dim(pair, core, axis=1, keepdims=False).sum(0)
    copies = call(line_kernel, shape(NY * NH, *slot), [VM], (swap(half, LINES),))
    outs = [shape(SLOTS, *NARROW, LANES)] + [shape(1, LANES)] * (slot[1] != JB)
    copies, *sums = call(plane_kernel, outs, [VM], (swap(copies, PLANES),))
    full = lax.all_gather(swap(copies, LINES), "all", axis=0, axis_index_groups=PAIRS)
    return full.reshape(TABLE, *NARROW, LANES), *sums


def local(sensitivity, tile_rows, tile_cols, tile_count, travel_times):
    tiles = sensitivity[0]
    lists = (tile_rows, tile_cols, tile_count)
    square = shape(LANES, LANES)
    columns = pltpu.VMEM((RB, LANES, LANES), jnp.float32)
    far = pl.BlockSpec(memory_space=pl.ANY)
    short = [pltpu.SMEM((1, TS), jnp.int32)] * 2

    table, times_t = call(
        first_kernel,
        [shape(TABLE, *NARROW, LANES), square],
        [far, far, SM, far, VM],
        (*lists, tiles, travel_times),
        [columns, columns, *short, pltpu.SemaphoreType.DMA((6,))],
        54528,
    )
    (cells,) = exchange(table)
    table, image_t = call(
        second_kernel,
        [shape(TABLE, *PAIRED, LANES), square],
        [far, far, SM] + [VM] * 3,
        (*lists, tiles, cells, times_t),
        [columns, *short, pltpu.SemaphoreType.DMA((2,))],
    )
    cells_2, sums = exchange(table)
    copies, held = call(
        third_kernel,
        [shape(NY * NX, 1, LANES), shape(6, 2, LANES)],
        [SM] * 3 + [VM] * 6,
        (*lists, tiles, cells, cells_2, times_t, image_t, sums),
    )
    rows = swap(copies, ALL_YX).sum(0)
    rows = swap(jnp.broadcast_to(rows[None], (NZ * NC, 1, LANES)), CHIPS_Z)
    update, ratio = call(last_kernel, [shape(2, LANES), shape(1, 1)], [VM] * 2, (rows, held))
    return update, ratio.reshape(1)


def solution(mesh):
    flat = Mesh(mesh.devices.reshape(-1), ("all",))
    every = P("all")
    return jax.shard_map(
        local, mesh=flat, in_specs=(every,) * 5, out_specs=(every, P()), check_vma=False
    )
```
